32 devices in a mesh: pipe: 2 (over core), ctx: 4 (over z), dp: 4 (over y, x).
Axes of the slice: x: 2, y: 2, z: 4, core: 2. Of those that a mesh axis runs over, the one named last changes fastest.
Arguments:
- queries: bfloat16 [2, 4, 512, 2048], P('pipe', 'dp', 'ctx'), may hold values from -6 to 6
- keys: bfloat16 [2, 4, 512, 2048], P('pipe', 'dp', 'ctx'), may hold values from -6 to 6
- values: bfloat16 [2, 4, 512, 2048], P('pipe', 'dp', 'ctx'), may hold values from -6 to 6
- upstream: bfloat16 [2, 4, 512, 2048], P('pipe', 'dp', 'ctx'), may hold values from -6 to 6
- gain: float32 [2, 2048], P('pipe', 'ctx'), may hold values from 0.1 to 1.9
Outputs:
- query_grad: bfloat16 [2, 4, 512, 2048], P('pipe', 'dp', 'ctx')
- key_grad: bfloat16 [2, 4, 512, 2048], P('pipe', 'dp', 'ctx')
- value_grad: bfloat16 [2, 4, 512, 2048], P('pipe', 'dp', 'ctx')
- gain_grad: float32 [2, 2048], P('pipe', 'ctx')
The draws below stay inside these ranges and needn't reach their ends.
All inputs are finite; a program needn't handle non-finite values.
Results may differ from the reference program's by a relative error of at most 0.007.
Values may be sent and summed in bfloat16 or wider, within the bound.
A program may use at most 64 MiB of HBM per device.

```python
import jax
import jax.numpy as jnp
from jax import lax

HEADS = 16
HEAD_DIM = 128
STRETCH = 128
WINDOW = 512
SEQ = 512
WIDTH = 2048
N_PIPE = 2
N_DP = 4


def level_of(own_key, extent, split, low, top_value):
    level, own = 1.0, jax.random.fold_in(own_key, 6)
    for dim, blocks in split:
        heights = jnp.exp(jax.random.uniform(jax.random.fold_in(own, dim), (blocks,), jnp.float32, low / len(split), top_value / len(split)))
        level = level * jnp.repeat(heights, extent[dim] // blocks).reshape([-1 if axis == dim else 1 for axis in range(len(extent))])
    return level


def noise(key, dims, width, bound, split=(), held_as=jnp.bfloat16):
    factor_of = level_of(key, dims, split, -0.22, 0.18) if split else 1.0
    array = jax.random.normal(key, dims, jnp.float32) * width * factor_of
    return jnp.minimum(jnp.maximum(array, -bound), bound).astype(held_as)


def setup_inputs(seed: int = 0) -> dict:
    key_list = jax.random.split(jax.random.key(seed), 6)
    return {
        "queries": noise(key_list[0], (N_PIPE, N_DP, SEQ, WIDTH), 1.0, 6.0, ((0, 2), (1, 4), (2, 4))),
        "keys": noise(key_list[1], (N_PIPE, N_DP, SEQ, WIDTH), 1.0, 6.0, ((0, 2), (1, 4), (2, 4))),
        "values": noise(key_list[2], (N_PIPE, N_DP, SEQ, WIDTH), 1.0, 6.0, ((0, 2), (1, 4), (2, 4))),
        "upstream": noise(key_list[3], (N_PIPE, N_DP, SEQ, WIDTH), 1.0, 6.0, ((0, 2), (1, 4), (2, 4))),
        "gain": jnp.clip(1.0 + 0.18 * jax.random.normal(key_list[4], (N_PIPE, WIDTH), jnp.float32), 0.1, 1.9),
    }


def contract(form, left, right):
    return jnp.einsum(form, left.astype(jnp.float32), right.astype(jnp.float32))

def shifted(tensor, amount):
    length = tensor.shape[0]
    amount = min(amount, length)
    filler = jnp.zeros((amount,) + tensor.shape[1:], tensor.dtype)
    return jnp.concatenate([filler, tensor[:length - amount]], axis=0)

def lifted(tensor, amount):
    length = tensor.shape[0]
    amount = min(amount, length)
    filler = jnp.zeros((amount,) + tensor.shape[1:], tensor.dtype)
    return jnp.concatenate([tensor[amount:], filler], axis=0)

def head_grads(queries, keys, values, grad_out, gain_row):
    blocks = queries.shape[0] // STRETCH
    reach_blocks = WINDOW // STRETCH
    query_blocks = queries.reshape(blocks, STRETCH, HEAD_DIM)
    key_blocks = keys.reshape(blocks, STRETCH, HEAD_DIM)
    value_blocks = values.reshape(blocks, STRETCH, HEAD_DIM)
    grad_blocks = grad_out.reshape(blocks, STRETCH, HEAD_DIM)
    kv_stretches = contract('csi,csj->cij', key_blocks, value_blocks)
    prefix = shifted(jnp.cumsum(kv_stretches, axis=0), 1)
    window_state = (prefix - shifted(prefix, reach_blocks - 1)).astype(jnp.bfloat16)
    rows_iota = lax.broadcasted_iota(jnp.int32, (STRETCH, STRETCH), 0)
    cols_iota = lax.broadcasted_iota(jnp.int32, (STRETCH, STRETCH), 1)
    near_mask = rows_iota >= cols_iota
    far_mask = rows_iota < cols_iota
    far_keys = shifted(key_blocks, reach_blocks)
    far_values = shifted(value_blocks, reach_blocks)
    near_scores = jnp.where(near_mask, contract('cik,cjk->cij', query_blocks, key_blocks), 0.0).astype(jnp.bfloat16)
    far_scores = jnp.where(far_mask, contract('cik,cjk->cij', query_blocks, far_keys), 0.0).astype(jnp.bfloat16)
    mixed_out = contract('cij,cjd->cid', near_scores, value_blocks) + contract('cij,cjd->cid', far_scores, far_values) + contract('cik,ckd->cid', query_blocks, window_state)
    inv_rms = lax.rsqrt(lax.optimization_barrier(jnp.mean(mixed_out * mixed_out, axis=-1, keepdims=True)) + 1e-06)
    normed = mixed_out * inv_rms
    grad_float = grad_blocks.astype(jnp.float32)
    gain_part = lax.optimization_barrier(jnp.sum(grad_float * normed, axis=(0, 1)))
    scaled = grad_float * gain_row
    out_grad = (inv_rms * (scaled - normed * lax.optimization_barrier(jnp.mean(scaled * normed, axis=-1, keepdims=True)))).astype(jnp.bfloat16)
    near_dscores = jnp.where(near_mask, contract('cid,cjd->cij', out_grad, value_blocks), 0.0).astype(jnp.bfloat16)
    far_dscores = jnp.where(far_mask, contract('cid,cjd->cij', out_grad, far_values), 0.0).astype(jnp.bfloat16)
    state_grad = contract('cik,cid->ckd', query_blocks, out_grad)
    later = lifted(jnp.flip(jnp.cumsum(jnp.flip(state_grad, 0), axis=0), 0), 1)
    kv_grad = (later - lifted(later, reach_blocks - 1)).astype(jnp.bfloat16)
    query_part = contract('cij,cjk->cik', near_dscores, key_blocks) + contract('cij,cjk->cik', far_dscores, far_keys) + contract('cid,ckd->cik', out_grad, window_state)
    key_part = contract('cij,cik->cjk', near_dscores, query_blocks) + lifted(contract('cij,cik->cjk', far_dscores, query_blocks), reach_blocks) + contract('cjd,ckd->cjk', value_blocks, kv_grad)
    value_part = contract('cij,cid->cjd', near_scores, out_grad) + lifted(contract('cij,cid->cjd', far_scores, out_grad), reach_blocks) + contract('cjk,ckd->cjd', key_blocks, kv_grad)
    total = blocks * STRETCH
    return (query_part.reshape(total, HEAD_DIM).astype(jnp.bfloat16), key_part.reshape(total, HEAD_DIM).astype(jnp.bfloat16), value_part.reshape(total, HEAD_DIM).astype(jnp.bfloat16), gain_part)

def reference(queries, keys, values, upstream, gain):
    incoming = jnp.roll(upstream, -1, axis=0)

    def per_section(tensor):
        return tensor.reshape(N_PIPE, N_DP, SEQ, HEADS, HEAD_DIM)
    gain_rows = gain.reshape(N_PIPE, HEADS, HEAD_DIM)
    over_heads = jax.vmap(head_grads, in_axes=(1, 1, 1, 1, 0), out_axes=(1, 1, 1, 0))
    over_seqs = jax.vmap(over_heads, in_axes=(0, 0, 0, 0, None), out_axes=0)

    def section_grads(section_items):
        head_results = over_seqs(*section_items)
        return (head_results[0], head_results[1], head_results[2], lax.optimization_barrier(jnp.sum(head_results[3], axis=0)))
    results = lax.map(section_grads, (per_section(queries), per_section(keys), per_section(values), per_section(incoming), gain_rows))

    def joined(tensor):
        return tensor.reshape(N_PIPE, N_DP, SEQ, HEADS * HEAD_DIM)
    return (joined(results[0]), joined(results[1]), joined(results[2]), results[3].reshape(N_PIPE, HEADS * HEAD_DIM))
```

```python
import functools

import jax
import jax.numpy as jnp
from jax import lax
from jax.experimental import pallas as pl
from jax.experimental.pallas import tpu as pltpu
from jax.sharding import PartitionSpec as P

HEAD_DIM = 128
STRETCH = 128
WINDOW = 512


def shifted_2(array, axis, by):
    devices = lax.axis_size(axis)
    return lax.ppermute(array, axis, [(i, (i + by) % devices) for i in range(devices)])


def contract(form, left, right):
    return jnp.einsum(form, left, right, preferred_element_type=jnp.float32)


def shifted(tensor, amount):
    length = tensor.shape[0]
    amount = min(amount, length)
    filler = jnp.zeros((amount,) + tensor.shape[1:], tensor.dtype)
    return jnp.concatenate([filler, tensor[: length - amount]], axis=0)


def lifted(tensor, amount):
    length = tensor.shape[0]
    amount = min(amount, length)
    filler = jnp.zeros((amount,) + tensor.shape[1:], tensor.dtype)
    return jnp.concatenate([tensor[amount:], filler], axis=0)


def local_grads(
    query_blocks,
    key_blocks,
    value_blocks,
    grad_blocks,
    far_keys,
    far_values,
    window_state,
    gain_rows,
):
    rows_iota = lax.broadcasted_iota(jnp.int32, (STRETCH, STRETCH), 0)
    cols_iota = lax.broadcasted_iota(jnp.int32, (STRETCH, STRETCH), 1)
    near_mask = rows_iota >= cols_iota
    far_mask = rows_iota < cols_iota
    near_scores = jnp.where(
        near_mask, contract("cihk,cjhk->chij", query_blocks, key_blocks), 0.0
    ).astype(jnp.bfloat16)
    far_scores = jnp.where(
        far_mask, contract("cihk,cjhk->chij", query_blocks, far_keys), 0.0
    ).astype(jnp.bfloat16)
    mixed_out = (
        contract("chij,cjhd->cihd", near_scores, value_blocks)
        + contract("chij,cjhd->cihd", far_scores, far_values)
        + contract("cihk,chkd->cihd", query_blocks, window_state)
    )
    inv_rms = lax.rsqrt(jnp.mean(mixed_out * mixed_out, axis=-1, keepdims=True) + 1e-06)
    normed = mixed_out * inv_rms
    grad_float = grad_blocks.astype(jnp.float32)
    gain_part = jnp.sum(grad_float * normed, axis=(0, 1))
    scaled = grad_float * gain_rows
    out_grad = (
        inv_rms * (scaled - normed * jnp.mean(scaled * normed, axis=-1, keepdims=True))
    ).astype(jnp.bfloat16)
    near_dscores = jnp.where(
        near_mask, contract("cihd,cjhd->chij", out_grad, value_blocks), 0.0
    ).astype(jnp.bfloat16)
    far_dscores = jnp.where(
        far_mask, contract("cihd,cjhd->chij", out_grad, far_values), 0.0
    ).astype(jnp.bfloat16)
    state_grad = contract("cihk,cihd->chkd", query_blocks, out_grad)
    query_part = (
        contract("chij,cjhk->cihk", near_dscores, key_blocks)
        + contract("chij,cjhk->cihk", far_dscores, far_keys)
        + contract("cihd,chkd->cihk", out_grad, window_state)
    )
    key_near = contract("chij,cihk->cjhk", near_dscores, query_blocks)
    key_far = contract("chij,cihk->cjhk", far_dscores, query_blocks)
    value_near = contract("chij,cihd->cjhd", near_scores, out_grad)
    value_far = contract("chij,cihd->cjhd", far_scores, out_grad)
    return (query_part, key_near, key_far, value_near, value_far, state_grad, gain_part)


def finish(
    query_part,
    key_near,
    key_far_here,
    value_near,
    value_far_here,
    key_blocks,
    value_blocks,
    kv_grad,
):
    key_part = key_near + key_far_here + contract("cjhd,chkd->cjhk", value_blocks, kv_grad)
    value_part = value_near + value_far_here + contract("cjhk,chkd->cjhd", key_blocks, kv_grad)
    return (
        query_part.astype(jnp.bfloat16),
        key_part.astype(jnp.bfloat16),
        value_part.astype(jnp.bfloat16),
    )


def blocked(tensor, heads_count):
    return tensor[0, 0].reshape(-1, STRETCH, heads_count, HEAD_DIM)


GROUP = 2
MESH = pl.DeviceIdType.MESH
NN = (((1,), (0,)), ((), ()))
NT = (((1,), (1,)), ((), ()))
TN = (((0,), (0,)), ((), ()))


def dot(left, right, dims):
    return lax.dot_general(left, right, dims, preferred_element_type=jnp.float32)


def chain_kernel(
    n_ctx,
    n_dp,
    q_ref,
    k_ref,
    v_ref,
    up_ref,
    gain_ref,
    qg_ref,
    kg_ref,
    vg_ref,
    gg_ref,
    g_buf,
    gain_all,
    gain_part,
    gain_stage,
    gain_mine,
    gain_final,
    kv_buf,
    near_buf,
    mix_buf,
    key_buf,
    val_buf,
    sg_buf,
    fwd_out,
    fwd_in,
    bwd_out,
    bwd_in,
    fwd_send,
    fwd_recv,
    bwd_send,
    bwd_recv,
    up_sem,
    gain_sem,
    stage_sem,
    final_sem,
):
    pipe = lax.axis_index("pipe")
    me = lax.axis_index("ctx")
    dp = lax.axis_index("dp")
    tokens, width = q_ref.shape
    heads = width // HEAD_DIM
    chunks = heads // GROUP
    per = width // n_ctx
    last = n_ctx - 1

    def at_ctx(c):
        return (pipe, c, dp)

    def at_dp(d):
        return (pipe, me, d)

    other = (1 - pipe, me, dp)
    ctx_peers = [lax.rem(me + o, n_ctx) for o in range(1, n_ctx)]
    dp_peers = [lax.rem(dp + o, n_dp) for o in range(1, n_dp)]

    barrier = pltpu.get_barrier_semaphore()
    pl.semaphore_signal(barrier, inc=1, device_id=other, device_id_type=MESH)
    for c in ctx_peers:
        pl.semaphore_signal(barrier, inc=1, device_id=at_ctx(c), device_id_type=MESH)
    for d in dp_peers:
        pl.semaphore_signal(barrier, inc=1, device_id=at_dp(d), device_id_type=MESH)

    def lanes(c, j):
        return pl.ds(pl.multiple_of((c * GROUP + j) * HEAD_DIM, HEAD_DIM), HEAD_DIM)

    def remote(src, dst, send, recv, target):
        return pltpu.make_async_remote_copy(
            src_ref=src,
            dst_ref=dst,
            send_sem=send,
            recv_sem=recv,
            device_id=target,
            device_id_type=MESH,
        )

    def fwd_copy(c):
        return remote(
            fwd_out.at[c],
            fwd_in.at[c],
            fwd_send.at[c],
            fwd_recv.at[c],
            at_ctx(jnp.minimum(me + 1, last)),
        )

    def bwd_copy(c):
        return remote(
            bwd_out.at[c],
            bwd_in.at[c],
            bwd_send.at[c],
            bwd_recv.at[c],
            at_ctx(jnp.maximum(me - 1, 0)),
        )

    @pl.when(me == 0)
    def _():
        fwd_in[...] = jnp.zeros_like(fwd_in)

    @pl.when(me == last)
    def _():
        bwd_in[...] = jnp.zeros_like(bwd_in)

    gain_all[me] = gain_ref[...]
    pl.semaphore_wait(barrier, 1 + len(ctx_peers) + len(dp_peers))

    def first(c, carry):
        for j in range(GROUP):
            at = lanes(c, j)
            kv = dot(k_ref[:, at], v_ref[:, at], TN)
            kv_buf[c, j] = kv
            fwd_out[c, j] = kv.astype(jnp.bfloat16)

        @pl.when(me == 0)
        def _():
            fwd_copy(c).start()

        return carry

    lax.fori_loop(0, chunks, first, 0)

    up_copy = remote(up_ref, g_buf, up_sem.at[0], up_sem.at[1], other)
    up_copy.start()
    gain_copies = []
    for o, c in enumerate(ctx_peers):
        copy = remote(
            gain_ref, gain_all.at[me], gain_sem.at[0, o], gain_sem.at[1, o], at_ctx(c)
        )
        copy.start()
        gain_copies.append(copy)

    rows = lax.broadcasted_iota(jnp.int32, (tokens, tokens), 0)
    cols = lax.broadcasted_iota(jnp.int32, (tokens, tokens), 1)
    mask = rows >= cols

    def second(c, carry):
        for j in range(GROUP):
            at = lanes(c, j)
            near = jnp.where(mask, dot(q_ref[:, at], k_ref[:, at], NT), 0.0)
            near = near.astype(jnp.bfloat16)
            near_buf[c, j] = near
            mix_buf[c, j] = dot(near, v_ref[:, at], NN)
        return carry

    lax.fori_loop(0, chunks, second, 0)

    up_copy.wait()
    for copy in gain_copies:
        copy.wait()

    def forward(c):
        @pl.when(me > 0)
        def _():
            fwd_copy(c).wait_recv()

        @pl.when(jnp.logical_and(me > 0, me < last))
        def _():
            for j in range(GROUP):
                total = kv_buf[c, j] + fwd_in[c, j].astype(jnp.float32)
                fwd_out[c, j] = total.astype(jnp.bfloat16)
            fwd_copy(c).start()

        later = []
        for j in range(GROUP):
            at = lanes(c, j)
            query, state = q_ref[:, at], fwd_in[c, j]
            mixed = mix_buf[c, j] + dot(query, state, NN)
            inv_rms = lax.rsqrt(jnp.mean(mixed * mixed, axis=-1, keepdims=True) + 1e-06)
            normed = mixed * inv_rms
            grad = g_buf[:, at].astype(jnp.float32)
            place = (c * GROUP + j) * HEAD_DIM
            owner = place // per
            inside = pl.ds(pl.multiple_of(lax.rem(place, per), HEAD_DIM), HEAD_DIM)
            product = grad * normed
            gain_part[owner, :, inside] = jnp.sum(product, axis=0, keepdims=True)
            gain_row = gain_all[owner, :, inside]
            pull = jnp.mean(product * gain_row, axis=-1, keepdims=True)
            mixed_grad = (inv_rms * (grad * gain_row - normed * pull)).astype(jnp.bfloat16)
            state_grad = dot(query, mixed_grad, TN)
            sg_buf[c, j] = state_grad
            bwd_out[c, j] = state_grad.astype(jnp.bfloat16)
            later.append((at, query, state, mixed_grad))

        @pl.when(me == last)
        def _():
            bwd_copy(c).start()

        for j, (at, query, state, mixed_grad) in enumerate(later):
            near_grad = jnp.where(mask, dot(mixed_grad, v_ref[:, at], NT), 0.0)
            near_grad = near_grad.astype(jnp.bfloat16)
            query_grad = dot(near_grad, k_ref[:, at], NN) + dot(mixed_grad, state, NT)
            qg_ref[:, at] = query_grad.astype(jnp.bfloat16)
            key_buf[c, j] = dot(near_grad, query, TN)
            val_buf[c, j] = dot(near_buf[c, j], mixed_grad, TN)

    def backward(c):
        @pl.when(me < last)
        def _():
            bwd_copy(c).wait_recv()

        @pl.when(jnp.logical_and(me > 0, me < last))
        def _():
            for j in range(GROUP):
                total = sg_buf[c, j] + bwd_in[c, j].astype(jnp.float32)
                bwd_out[c, j] = total.astype(jnp.bfloat16)
            bwd_copy(c).start()

        for j in range(GROUP):
            at = lanes(c, j)
            kv_grad = bwd_in[c, j]
            key_grad = key_buf[c, j] + dot(v_ref[:, at], kv_grad, NT)
            kg_ref[:, at] = key_grad.astype(jnp.bfloat16)
            val_grad = val_buf[c, j] + dot(k_ref[:, at], kv_grad, NN)
            vg_ref[:, at] = val_grad.astype(jnp.bfloat16)

    def stage_copy(o):
        c = ctx_peers[o]
        return remote(
            gain_part.at[c], gain_stage.at[o], stage_sem.at[0, o], stage_sem.at[1, o], at_ctx(c)
        )

    def final_copy(o):
        return remote(
            gain_mine, gain_final.at[o], final_sem.at[0, o], final_sem.at[1, o], at_dp(dp_peers[o])
        )

    lag = jnp.minimum(chunks, (last - me) * LAG)
    steps = chunks + min(chunks, last * LAG)

    def step(i, carry):
        @pl.when(i < chunks)
        def _():
            forward(i)

        @pl.when(i == chunks - 1)
        def _():
            for o in range(n_ctx - 1):
                stage_copy(o).start()

        @pl.when(i == steps - 2)
        def _():
            total = gain_part[me]
            for o in range(n_ctx - 1):
                stage_copy(o).wait()
                total = total + gain_stage[o]
            gain_mine[...] = total
            for o in range(n_dp - 1):
                final_copy(o).start()

        @pl.when(jnp.logical_and(i >= lag, i - lag < chunks))
        def _():
            backward(i - lag)

        return carry

    lax.fori_loop(0, steps, step, 0)

    total = gain_mine[...]
    for o in range(n_dp - 1):
        final_copy(o).wait()
        total = total + gain_final[o]
    gg_ref[...] = total

    @pl.when(me < last)
    def _():
        for c in range(chunks):
            fwd_copy(c).wait_send()

    @pl.when(me > 0)
    def _():
        for c in range(chunks):
            bwd_copy(c).wait_send()


LAG = 4


def chained(queries, keys, values, upstream, gain):
    n_ctx, n_dp = lax.axis_size("ctx"), lax.axis_size("dp")
    tokens, width = queries.shape[2:]
    heads = width // HEAD_DIM
    chunks = heads // GROUP
    per = gain.shape[1]
    wide = (chunks, GROUP, HEAD_DIM, HEAD_DIM)
    rows = (chunks, GROUP, tokens, HEAD_DIM)
    dma = pltpu.SemaphoreType.DMA
    vmem = pl.BlockSpec(memory_space=pltpu.VMEM)
    token_out = jax.ShapeDtypeStruct((tokens, width), jnp.bfloat16)
    flat = [x.reshape(tokens, width) for x in (queries, keys, values, upstream)]
    query_grad, key_grad, value_grad, gain_grad = pl.pallas_call(
        functools.partial(chain_kernel, n_ctx, n_dp),
        out_shape=(token_out, token_out, token_out, jax.ShapeDtypeStruct((1, per), jnp.float32)),
        in_specs=[vmem] * 5,
        out_specs=(vmem,) * 4,
        scratch_shapes=[
            pltpu.VMEM((tokens, width), jnp.bfloat16),
            pltpu.VMEM((n_ctx, 1, per), jnp.float32),
            pltpu.VMEM((n_ctx, 1, per), jnp.float32),
            pltpu.VMEM((n_ctx, 1, per), jnp.float32),
            pltpu.VMEM((1, per), jnp.float32),
            pltpu.VMEM((n_dp, 1, per), jnp.float32),
            pltpu.VMEM(wide, jnp.float32),
            pltpu.VMEM((chunks, GROUP, tokens, tokens), jnp.bfloat16),
            pltpu.VMEM(rows, jnp.float32),
            pltpu.VMEM(rows, jnp.float32),
            pltpu.VMEM(rows, jnp.float32),
            pltpu.VMEM(wide, jnp.float32),
            pltpu.VMEM(wide, jnp.bfloat16),
            pltpu.VMEM(wide, jnp.bfloat16),
            pltpu.VMEM(wide, jnp.bfloat16),
            pltpu.VMEM(wide, jnp.bfloat16),
            dma((chunks,)),
            dma((chunks,)),
            dma((chunks,)),
            dma((chunks,)),
            dma((2,)),
            dma((2, n_ctx)),
            dma((2, n_ctx)),
            dma((2, n_dp)),
        ],
        compiler_params=pltpu.CompilerParams(
            collective_id=0, has_side_effects=True, vmem_limit_bytes=40 * 1024 * 1024
        ),
    )(*flat, gain)
    shape = queries.shape
    return (
        query_grad.reshape(shape),
        key_grad.reshape(shape),
        value_grad.reshape(shape),
        gain_grad,
    )


def shards(queries, keys, values, upstream, gain):
    reach_blocks = WINDOW // STRETCH
    if (
        queries.shape[2] == STRETCH
        and 1 < lax.axis_size("ctx") <= reach_blocks
        and lax.axis_size("pipe") == 2
    ):
        return chained(queries, keys, values, upstream, gain)
    incoming = shifted_2(upstream, "pipe", -1)
    heads_here = gain.shape[1] // HEAD_DIM
    query_heads, key_heads, value_heads, grad_heads = (
        lax.all_to_all(queries, "ctx", split_axis=3, concat_axis=2, tiled=True),
        lax.all_to_all(keys, "ctx", split_axis=3, concat_axis=2, tiled=True),
        lax.all_to_all(values, "ctx", split_axis=3, concat_axis=2, tiled=True),
        lax.all_to_all(incoming, "ctx", split_axis=3, concat_axis=2, tiled=True),
    )
    seq_len = query_heads.shape[2]
    gain_rows = gain[0].reshape(heads_here, HEAD_DIM)
    query_blocks = blocked(query_heads, heads_here)
    key_blocks = blocked(key_heads, heads_here)
    value_blocks = blocked(value_heads, heads_here)
    grad_blocks = blocked(grad_heads, heads_here)
    kv_stretches = contract("cshi,cshj->chij", key_blocks, value_blocks)
    prefix = shifted(jnp.cumsum(kv_stretches, axis=0), 1)
    window_state = (prefix - shifted(prefix, reach_blocks - 1)).astype(jnp.bfloat16)
    far_keys = shifted(key_blocks, reach_blocks)
    far_values = shifted(value_blocks, reach_blocks)
    query_part, key_near, key_far, value_near, value_far, state_grad, gain_part = local_grads(
        query_blocks,
        key_blocks,
        value_blocks,
        grad_blocks,
        far_keys,
        far_values,
        window_state,
        gain_rows,
    )
    later = lifted(jnp.flip(jnp.cumsum(jnp.flip(state_grad, 0), axis=0), 0), 1)
    kv_grad = (later - lifted(later, reach_blocks - 1)).astype(jnp.bfloat16)
    query_out, key_out, value_out = finish(
        query_part,
        key_near,
        lifted(key_far, reach_blocks),
        value_near,
        lifted(value_far, reach_blocks),
        key_blocks,
        value_blocks,
        kv_grad,
    )

    def head_rows(tensor):
        return tensor.reshape(1, 1, seq_len, heads_here * HEAD_DIM)

    query_grad, key_grad, value_grad = (
        lax.all_to_all(head_rows(query_out), "ctx", split_axis=2, concat_axis=3, tiled=True),
        lax.all_to_all(head_rows(key_out), "ctx", split_axis=2, concat_axis=3, tiled=True),
        lax.all_to_all(head_rows(value_out), "ctx", split_axis=2, concat_axis=3, tiled=True),
    )
    gain_share = gain_part.reshape(1, heads_here * HEAD_DIM)
    gain_total = lax.psum(gain_share, "dp")
    return (query_grad, key_grad, value_grad, gain_total)


def solution(mesh):
    in_specs = (
        P("pipe", "dp", "ctx", None),
        P("pipe", "dp", "ctx", None),
        P("pipe", "dp", "ctx", None),
        P("pipe", "dp", "ctx", None),
        P("pipe", "ctx"),
    )
    out_specs = (
        P("pipe", "dp", "ctx", None),
        P("pipe", "dp", "ctx", None),
        P("pipe", "dp", "ctx", None),
        P("pipe", "ctx"),
    )
    return jax.shard_map(shards, mesh=mesh, in_specs=in_specs, out_specs=out_specs, check_vma=False)
```

```python
import functools

import jax
import jax.numpy as jnp
from jax import lax
from jax.experimental import pallas as pl
from jax.experimental.pallas import tpu as pltpu
from jax.sharding import PartitionSpec as P

HEAD_DIM = 128
STRETCH = 128
WINDOW = 512


def shifted_2(array, axis, by):
    devices = lax.axis_size(axis)
    return lax.ppermute(array, axis, [(i, (i + by) % devices) for i in range(devices)])


def contract(form, left, right):
    return jnp.einsum(form, left, right, preferred_element_type=jnp.float32)


def shifted(tensor, amount):
    length = tensor.shape[0]
    amount = min(amount, length)
    filler = jnp.zeros((amount,) + tensor.shape[1:], tensor.dtype)
    return jnp.concatenate([filler, tensor[: length - amount]], axis=0)


def lifted(tensor, amount):
    length = tensor.shape[0]
    amount = min(amount, length)
    filler = jnp.zeros((amount,) + tensor.shape[1:], tensor.dtype)
    return jnp.concatenate([tensor[amount:], filler], axis=0)


def local_grads(
    query_blocks,
    key_blocks,
    value_blocks,
    grad_blocks,
    far_keys,
    far_values,
    window_state,
    gain_rows,
):
    rows_iota = lax.broadcasted_iota(jnp.int32, (STRETCH, STRETCH), 0)
    cols_iota = lax.broadcasted_iota(jnp.int32, (STRETCH, STRETCH), 1)
    near_mask = rows_iota >= cols_iota
    far_mask = rows_iota < cols_iota
    near_scores = jnp.where(
        near_mask, contract("cihk,cjhk->chij", query_blocks, key_blocks), 0.0
    ).astype(jnp.bfloat16)
    far_scores = jnp.where(
        far_mask, contract("cihk,cjhk->chij", query_blocks, far_keys), 0.0
    ).astype(jnp.bfloat16)
    mixed_out = (
        contract("chij,cjhd->cihd", near_scores, value_blocks)
        + contract("chij,cjhd->cihd", far_scores, far_values)
        + contract("cihk,chkd->cihd", query_blocks, window_state)
    )
    inv_rms = lax.rsqrt(jnp.mean(mixed_out * mixed_out, axis=-1, keepdims=True) + 1e-06)
    normed = mixed_out * inv_rms
    grad_float = grad_blocks.astype(jnp.float32)
    gain_part = jnp.sum(grad_float * normed, axis=(0, 1))
    scaled = grad_float * gain_rows
    out_grad = (
        inv_rms * (scaled - normed * jnp.mean(scaled * normed, axis=-1, keepdims=True))
    ).astype(jnp.bfloat16)
    near_dscores = jnp.where(
        near_mask, contract("cihd,cjhd->chij", out_grad, value_blocks), 0.0
    ).astype(jnp.bfloat16)
    far_dscores = jnp.where(
        far_mask, contract("cihd,cjhd->chij", out_grad, far_values), 0.0
    ).astype(jnp.bfloat16)
    state_grad = contract("cihk,cihd->chkd", query_blocks, out_grad)
    query_part = (
        contract("chij,cjhk->cihk", near_dscores, key_blocks)
        + contract("chij,cjhk->cihk", far_dscores, far_keys)
        + contract("cihd,chkd->cihk", out_grad, window_state)
    )
    key_near = contract("chij,cihk->cjhk", near_dscores, query_blocks)
    key_far = contract("chij,cihk->cjhk", far_dscores, query_blocks)
    value_near = contract("chij,cihd->cjhd", near_scores, out_grad)
    value_far = contract("chij,cihd->cjhd", far_scores, out_grad)
    return (query_part, key_near, key_far, value_near, value_far, state_grad, gain_part)


def finish(
    query_part,
    key_near,
    key_far_here,
    value_near,
    value_far_here,
    key_blocks,
    value_blocks,
    kv_grad,
):
    key_part = key_near + key_far_here + contract("cjhd,chkd->cjhk", value_blocks, kv_grad)
    value_part = value_near + value_far_here + contract("cjhk,chkd->cjhd", key_blocks, kv_grad)
    return (
        query_part.astype(jnp.bfloat16),
        key_part.astype(jnp.bfloat16),
        value_part.astype(jnp.bfloat16),
    )


def blocked(tensor, heads_count):
    return tensor[0, 0].reshape(-1, STRETCH, heads_count, HEAD_DIM)


GROUP = 2
MESH = pl.DeviceIdType.MESH
NN = (((1,), (0,)), ((), ()))
NT = (((1,), (1,)), ((), ()))
TN = (((0,), (0,)), ((), ()))


def dot(left, right, dims):
    return lax.dot_general(left, right, dims, preferred_element_type=jnp.float32)


def chain_kernel(
    n_ctx,
    n_dp,
    q_hbm,
    k_hbm,
    v_hbm,
    up_ref,
    gain_ref,
    qg_hbm,
    kg_hbm,
    vg_hbm,
    gg_ref,
    qg_ref,
    kg_ref,
    vg_ref,
    q_ref,
    k_ref,
    v_ref,
    g_buf,
    gain_all,
    gain_part,
    gain_stage,
    gain_mine,
    gain_final,
    kv_buf,
    near_buf,
    mix_buf,
    key_buf,
    val_buf,
    sg_buf,
    fwd_out,
    fwd_in,
    bwd_out,
    bwd_in,
    fwd_send,
    fwd_recv,
    bwd_send,
    bwd_recv,
    load_sem,
    store_sem,
    up_sem,
    gain_sem,
    stage_sem,
    final_sem,
):
    loads = [
        pltpu.make_async_copy(src, dst, load_sem.at[i])
        for i, (src, dst) in enumerate(((k_hbm, k_ref), (v_hbm, v_ref), (q_hbm, q_ref)))
    ]
    for load in loads:
        load.start()
    pipe = lax.axis_index("pipe")
    me = lax.axis_index("ctx")
    dp = lax.axis_index("dp")
    tokens, width = q_ref.shape
    heads = width // HEAD_DIM
    chunks = heads // GROUP
    per = width // n_ctx
    last = n_ctx - 1

    def at_ctx(c):
        return (pipe, c, dp)

    def at_dp(d):
        return (pipe, me, d)

    other = (1 - pipe, me, dp)
    ctx_peers = [lax.rem(me + o, n_ctx) for o in range(1, n_ctx)]
    dp_peers = [lax.rem(dp + o, n_dp) for o in range(1, n_dp)]

    barrier = pltpu.get_barrier_semaphore()
    pl.semaphore_signal(barrier, inc=1, device_id=other, device_id_type=MESH)
    for c in ctx_peers:
        pl.semaphore_signal(barrier, inc=1, device_id=at_ctx(c), device_id_type=MESH)
    for d in dp_peers:
        pl.semaphore_signal(barrier, inc=1, device_id=at_dp(d), device_id_type=MESH)

    def lanes(c, j):
        return pl.ds(pl.multiple_of((c * GROUP + j) * HEAD_DIM, HEAD_DIM), HEAD_DIM)

    def remote(src, dst, send, recv, target):
        return pltpu.make_async_remote_copy(
            src_ref=src,
            dst_ref=dst,
            send_sem=send,
            recv_sem=recv,
            device_id=target,
            device_id_type=MESH,
        )

    def fwd_copy(c, j):
        return remote(
            fwd_out.at[c, j],
            fwd_in.at[c, j],
            fwd_send.at[c, j],
            fwd_recv.at[c, j],
            at_ctx(jnp.minimum(me + 1, last)),
        )

    def bwd_copy(c, j):
        return remote(
            bwd_out.at[c, j],
            bwd_in.at[c, j],
            bwd_send.at[c, j],
            bwd_recv.at[c, j],
            at_ctx(jnp.maximum(me - 1, 0)),
        )

    @pl.when(me == 0)
    def _():
        fwd_in[...] = jnp.zeros_like(fwd_in)

    @pl.when(me == last)
    def _():
        bwd_in[...] = jnp.zeros_like(bwd_in)

    own_gain = pltpu.make_async_copy(gain_ref, gain_all.at[me], load_sem.at[3])
    own_gain.start()
    loads[0].wait()
    loads[1].wait()
    pl.semaphore_wait(barrier, 1 + len(ctx_peers) + len(dp_peers))

    def first(c, carry):
        for j in range(GROUP):
            at = lanes(c, j)
            kv = dot(k_ref[:, at], v_ref[:, at], TN)
            kv_buf[c, j] = kv
            fwd_out[c, j] = kv.astype(jnp.bfloat16)

        @pl.when(me == 0)
        def _():
            for j in range(GROUP):
                fwd_copy(c, j).start()

        return carry

    lax.fori_loop(0, chunks, first, 0)

    up_copy = remote(up_ref, g_buf, up_sem.at[0], up_sem.at[1], other)
    up_copy.start()
    gain_copies = []
    for o, c in enumerate(ctx_peers):
        copy = remote(
            gain_ref, gain_all.at[me], gain_sem.at[0, o], gain_sem.at[1, o], at_ctx(c)
        )
        copy.start()
        gain_copies.append(copy)

    loads[2].wait()
    own_gain.wait()
    rows = lax.broadcasted_iota(jnp.int32, (tokens, tokens), 0)
    cols = lax.broadcasted_iota(jnp.int32, (tokens, tokens), 1)
    mask = rows >= cols

    def second(c, carry):
        for j in range(GROUP):
            at = lanes(c, j)
            near = jnp.where(mask, dot(q_ref[:, at], k_ref[:, at], NT), 0.0)
            near = near.astype(jnp.bfloat16)
            near_buf[c, j] = near
            mix_buf[c, j] = dot(near, v_ref[:, at], NN)
        return carry

    lax.fori_loop(0, chunks, second, 0)

    up_copy.wait()
    for copy in gain_copies:
        copy.wait()

    def store(which, c):
        source = (qg_ref, kg_ref, vg_ref)[which]
        target = (qg_hbm, kg_hbm, vg_hbm)[which]
        wide = GROUP * HEAD_DIM
        at = pl.ds(pl.multiple_of(c * wide, wide), wide)
        return pltpu.make_async_copy(source.at[:, at], target.at[:, at], store_sem.at[which, c])

    def forward(c):
        @pl.when(me == last)
        def _():
            for j in range(GROUP):
                fwd_copy(c, j).wait_recv()

        @pl.when(jnp.logical_and(me > 0, me < last))
        def _():
            for j in range(GROUP):
                fwd_copy(c, j).wait_recv()
                total = kv_buf[c, j] + fwd_in[c, j].astype(jnp.float32)
                fwd_out[c, j] = total.astype(jnp.bfloat16)
                fwd_copy(c, j).start()

        later = []
        for j in range(GROUP):
            at = lanes(c, j)
            query, state = q_ref[:, at], fwd_in[c, j]
            mixed = mix_buf[c, j] + dot(query, state, NN)
            inv_rms = lax.rsqrt(jnp.mean(mixed * mixed, axis=-1, keepdims=True) + 1e-06)
            normed = mixed * inv_rms
            grad = g_buf[:, at].astype(jnp.float32)
            place = (c * GROUP + j) * HEAD_DIM
            owner = place // per
            inside = pl.ds(pl.multiple_of(lax.rem(place, per), HEAD_DIM), HEAD_DIM)
            product = grad * normed
            gain_part[owner, :, inside] = jnp.sum(product, axis=0, keepdims=True)
            gain_row = gain_all[owner, :, inside]
            pull = jnp.mean(product * gain_row, axis=-1, keepdims=True)
            mixed_grad = (inv_rms * (grad * gain_row - normed * pull)).astype(jnp.bfloat16)
            state_grad = dot(query, mixed_grad, TN)
            sg_buf[c, j] = state_grad
            bwd_out[c, j] = state_grad.astype(jnp.bfloat16)
            later.append((at, query, state, mixed_grad))

        @pl.when(me == last)
        def _():
            for j in range(GROUP):
                bwd_copy(c, j).start()

        for j, (at, query, state, mixed_grad) in enumerate(later):
            near_grad = jnp.where(mask, dot(mixed_grad, v_ref[:, at], NT), 0.0)
            near_grad = near_grad.astype(jnp.bfloat16)
            query_grad = dot(near_grad, k_ref[:, at], NN) + dot(mixed_grad, state, NT)
            qg_ref[:, at] = query_grad.astype(jnp.bfloat16)
            key_buf[c, j] = dot(near_grad, query, TN)
            val_buf[c, j] = dot(near_buf[c, j], mixed_grad, TN)
        store(0, c).start()

    def backward(c):
        @pl.when(me == 0)
        def _():
            for j in range(GROUP):
                bwd_copy(c, j).wait_recv()

        @pl.when(jnp.logical_and(me > 0, me < last))
        def _():
            for j in range(GROUP):
                bwd_copy(c, j).wait_recv()
                total = sg_buf[c, j] + bwd_in[c, j].astype(jnp.float32)
                bwd_out[c, j] = total.astype(jnp.bfloat16)
                bwd_copy(c, j).start()

        for j in range(GROUP):
            at = lanes(c, j)
            kv_grad = bwd_in[c, j]
            key_grad = key_buf[c, j] + dot(v_ref[:, at], kv_grad, NT)
            kg_ref[:, at] = key_grad.astype(jnp.bfloat16)
            val_grad = val_buf[c, j] + dot(k_ref[:, at], kv_grad, NN)
            vg_ref[:, at] = val_grad.astype(jnp.bfloat16)
        store(1, c).start()
        store(2, c).start()

    def stage_copy(o):
        c = ctx_peers[o]
        return remote(
            gain_part.at[c], gain_stage.at[o], stage_sem.at[0, o], stage_sem.at[1, o], at_ctx(c)
        )

    def final_copy(o):
        return remote(
            gain_mine, gain_final.at[o], final_sem.at[0, o], final_sem.at[1, o], at_dp(dp_peers[o])
        )

    lag = jnp.minimum(chunks, (last - me) * LAG)
    steps = chunks + min(chunks, last * LAG)

    def step(i, carry):
        @pl.when(i < chunks)
        def _():
            forward(i)

        @pl.when(i == chunks - 1)
        def _():
            for o in range(n_ctx - 1):
                stage_copy(o).start()

        @pl.when(i == steps - 3)
        def _():
            total = gain_part[me]
            for o in range(n_ctx - 1):
                stage_copy(o).wait()
                total = total + gain_stage[o]
            gain_mine[...] = total
            for o in range(n_dp - 1):
                final_copy(o).start()

        @pl.when(jnp.logical_and(i >= lag, i - lag < chunks))
        def _():
            backward(i - lag)

        return carry

    lax.fori_loop(0, steps, step, 0)

    total = gain_mine[...]
    for o in range(n_dp - 1):
        final_copy(o).wait()
        total = total + gain_final[o]
    gain_mine[...] = total
    out_gain = pltpu.make_async_copy(gain_mine, gg_ref, load_sem.at[4])
    out_gain.start()
    for c in range(chunks):
        for which in range(3):
            store(which, c).wait()
    out_gain.wait()

    @pl.when(me < last)
    def _():
        for c in range(chunks):
            for j in range(GROUP):
                fwd_copy(c, j).wait_send()

    @pl.when(me > 0)
    def _():
        for c in range(chunks):
            for j in range(GROUP):
                bwd_copy(c, j).wait_send()


LAG = 4
VMEM_BYTES = 63 * 1024 * 1024
PIECES = 4


def store_kernel(*refs):
    sources, targets, held, in_sems, out_sems = refs[:4], refs[4:8], refs[8:12], refs[12], refs[13]
    inward, outward = [], []
    for i in range(4):
        rows = sources[i].shape[0]
        pieces = PIECES if rows % (16 * PIECES) == 0 else 1
        for p in range(pieces):
            at = pl.ds(p * (rows // pieces), rows // pieces)
            here = held[i].at[at]
            inward.append(pltpu.make_async_copy(sources[i].at[at], here, in_sems.at[i, p]))
            outward.append(pltpu.make_async_copy(here, targets[i].at[at], out_sems.at[i, p]))
    for copy in inward:
        copy.start()
    for arrived, copy in zip(inward, outward):
        arrived.wait()
        copy.start()
    for copy in outward:
        copy.wait()


def chained(queries, keys, values, upstream, gain):
    n_ctx, n_dp = lax.axis_size("ctx"), lax.axis_size("dp")
    tokens, width = queries.shape[2:]
    heads = width // HEAD_DIM
    chunks = heads // GROUP
    per = gain.shape[1]
    wide = (chunks, GROUP, HEAD_DIM, HEAD_DIM)
    rows = (chunks, GROUP, tokens, HEAD_DIM)
    dma = pltpu.SemaphoreType.DMA
    token_out = jax.ShapeDtypeStruct((tokens, width), jnp.bfloat16)
    flat = [x.reshape(tokens, width) for x in (queries, keys, values, upstream)]
    hbm = pl.BlockSpec(memory_space=pltpu.HBM)
    shapes = (token_out, token_out, token_out, jax.ShapeDtypeStruct((1, per), jnp.float32))
    grads = pl.pallas_call(
        functools.partial(chain_kernel, n_ctx, n_dp),
        out_shape=shapes,
        in_specs=[hbm] * 5,
        out_specs=(hbm,) * 4,
        scratch_shapes=[
            pltpu.VMEM((tokens, width), jnp.bfloat16),
            pltpu.VMEM((tokens, width), jnp.bfloat16),
            pltpu.VMEM((tokens, width), jnp.bfloat16),
            pltpu.VMEM((tokens, width), jnp.bfloat16),
            pltpu.VMEM((tokens, width), jnp.bfloat16),
            pltpu.VMEM((tokens, width), jnp.bfloat16),
            pltpu.VMEM((tokens, width), jnp.bfloat16),
            pltpu.VMEM((n_ctx, 1, per), jnp.float32),
            pltpu.VMEM((n_ctx, 1, per), jnp.float32),
            pltpu.VMEM((n_ctx, 1, per), jnp.float32),
            pltpu.VMEM((1, per), jnp.float32),
            pltpu.VMEM((n_dp, 1, per), jnp.float32),
            pltpu.VMEM(wide, jnp.float32),
            pltpu.VMEM((chunks, GROUP, tokens, tokens), jnp.bfloat16),
            pltpu.VMEM(rows, jnp.float32),
            pltpu.VMEM(rows, jnp.float32),
            pltpu.VMEM(rows, jnp.float32),
            pltpu.VMEM(wide, jnp.float32),
            pltpu.VMEM(wide, jnp.bfloat16),
            pltpu.VMEM(wide, jnp.bfloat16),
            pltpu.VMEM(wide, jnp.bfloat16),
            pltpu.VMEM(wide, jnp.bfloat16),
            dma((chunks, GROUP)),
            dma((chunks, GROUP)),
            dma((chunks, GROUP)),
            dma((chunks, GROUP)),
            dma((5,)),
            dma((3, chunks)),
            dma((2,)),
            dma((2, n_ctx)),
            dma((2, n_ctx)),
            dma((2, n_dp)),
        ],
        compiler_params=pltpu.CompilerParams(
            collective_id=0, has_side_effects=True, vmem_limit_bytes=VMEM_BYTES
        ),
    )(*flat, gain)
    query_grad, key_grad, value_grad, gain_grad = pl.pallas_call(
        store_kernel,
        out_shape=shapes,
        in_specs=[hbm] * 4,
        out_specs=(hbm,) * 4,
        scratch_shapes=[pltpu.VMEM(x.shape, x.dtype) for x in shapes]
        + [dma((4, PIECES)), dma((4, PIECES))],
        compiler_params=pltpu.CompilerParams(vmem_limit_bytes=VMEM_BYTES),
    )(*grads)
    shape = queries.shape
    return (
        query_grad.reshape(shape),
        key_grad.reshape(shape),
        value_grad.reshape(shape),
        gain_grad,
    )


def shards(queries, keys, values, upstream, gain):
    reach_blocks = WINDOW // STRETCH
    if (
        queries.shape[2] == STRETCH
        and 1 < lax.axis_size("ctx") <= reach_blocks
        and lax.axis_size("pipe") == 2
    ):
        return chained(queries, keys, values, upstream, gain)
    incoming = shifted_2(upstream, "pipe", -1)
    heads_here = gain.shape[1] // HEAD_DIM
    query_heads, key_heads, value_heads, grad_heads = (
        lax.all_to_all(queries, "ctx", split_axis=3, concat_axis=2, tiled=True),
        lax.all_to_all(keys, "ctx", split_axis=3, concat_axis=2, tiled=True),
        lax.all_to_all(values, "ctx", split_axis=3, concat_axis=2, tiled=True),
        lax.all_to_all(incoming, "ctx", split_axis=3, concat_axis=2, tiled=True),
    )
    seq_len = query_heads.shape[2]
    gain_rows = gain[0].reshape(heads_here, HEAD_DIM)
    query_blocks = blocked(query_heads, heads_here)
    key_blocks = blocked(key_heads, heads_here)
    value_blocks = blocked(value_heads, heads_here)
    grad_blocks = blocked(grad_heads, heads_here)
    kv_stretches = contract("cshi,cshj->chij", key_blocks, value_blocks)
    prefix = shifted(jnp.cumsum(kv_stretches, axis=0), 1)
    window_state = (prefix - shifted(prefix, reach_blocks - 1)).astype(jnp.bfloat16)
    far_keys = shifted(key_blocks, reach_blocks)
    far_values = shifted(value_blocks, reach_blocks)
    query_part, key_near, key_far, value_near, value_far, state_grad, gain_part = local_grads(
        query_blocks,
        key_blocks,
        value_blocks,
        grad_blocks,
        far_keys,
        far_values,
        window_state,
        gain_rows,
    )
    later = lifted(jnp.flip(jnp.cumsum(jnp.flip(state_grad, 0), axis=0), 0), 1)
    kv_grad = (later - lifted(later, reach_blocks - 1)).astype(jnp.bfloat16)
    query_out, key_out, value_out = finish(
        query_part,
        key_near,
        lifted(key_far, reach_blocks),
        value_near,
        lifted(value_far, reach_blocks),
        key_blocks,
        value_blocks,
        kv_grad,
    )

    def head_rows(tensor):
        return tensor.reshape(1, 1, seq_len, heads_here * HEAD_DIM)

    query_grad, key_grad, value_grad = (
        lax.all_to_all(head_rows(query_out), "ctx", split_axis=2, concat_axis=3, tiled=True),
        lax.all_to_all(head_rows(key_out), "ctx", split_axis=2, concat_axis=3, tiled=True),
        lax.all_to_all(head_rows(value_out), "ctx", split_axis=2, concat_axis=3, tiled=True),
    )
    gain_share = gain_part.reshape(1, heads_here * HEAD_DIM)
    gain_total = lax.psum(gain_share, "dp")
    return (query_grad, key_grad, value_grad, gain_total)


def solution(mesh):
    in_specs = (
        P("pipe", "dp", "ctx", None),
        P("pipe", "dp", "ctx", None),
        P("pipe", "dp", "ctx", None),
        P("pipe", "dp", "ctx", None),
        P("pipe", "ctx"),
    )
    out_specs = (
        P("pipe", "dp", "ctx", None),
        P("pipe", "dp", "ctx", None),
        P("pipe", "dp", "ctx", None),
        P("pipe", "ctx"),
    )
    return jax.shard_map(shards, mesh=mesh, in_specs=in_specs, out_specs=out_specs, check_vma=False)
```

```python
import functools

import jax
import jax.numpy as jnp
from jax import lax
from jax.experimental import pallas as pl
from jax.experimental.pallas import tpu as pltpu
from jax.sharding import PartitionSpec as P

HEAD_DIM = 128
STRETCH = 128
WINDOW = 512


def shifted_2(array, axis, by):
    devices = lax.axis_size(axis)
    return lax.ppermute(array, axis, [(i, (i + by) % devices) for i in range(devices)])


def contract(form, left, right):
    return jnp.einsum(form, left, right, preferred_element_type=jnp.float32)


def shifted(tensor, amount):
    length = tensor.shape[0]
    amount = min(amount, length)
    filler = jnp.zeros((amount,) + tensor.shape[1:], tensor.dtype)
    return jnp.concatenate([filler, tensor[: length - amount]], axis=0)


def lifted(tensor, amount):
    length = tensor.shape[0]
    amount = min(amount, length)
    filler = jnp.zeros((amount,) + tensor.shape[1:], tensor.dtype)
    return jnp.concatenate([tensor[amount:], filler], axis=0)


def local_grads(
    query_blocks,
    key_blocks,
    value_blocks,
    grad_blocks,
    far_keys,
    far_values,
    window_state,
    gain_rows,
):
    rows_iota = lax.broadcasted_iota(jnp.int32, (STRETCH, STRETCH), 0)
    cols_iota = lax.broadcasted_iota(jnp.int32, (STRETCH, STRETCH), 1)
    near_mask = rows_iota >= cols_iota
    far_mask = rows_iota < cols_iota
    near_scores = jnp.where(
        near_mask, contract("cihk,cjhk->chij", query_blocks, key_blocks), 0.0
    ).astype(jnp.bfloat16)
    far_scores = jnp.where(
        far_mask, contract("cihk,cjhk->chij", query_blocks, far_keys), 0.0
    ).astype(jnp.bfloat16)
    mixed_out = (
        contract("chij,cjhd->cihd", near_scores, value_blocks)
        + contract("chij,cjhd->cihd", far_scores, far_values)
        + contract("cihk,chkd->cihd", query_blocks, window_state)
    )
    inv_rms = lax.rsqrt(jnp.mean(mixed_out * mixed_out, axis=-1, keepdims=True) + 1e-06)
    normed = mixed_out * inv_rms
    grad_float = grad_blocks.astype(jnp.float32)
    gain_part = jnp.sum(grad_float * normed, axis=(0, 1))
    scaled = grad_float * gain_rows
    out_grad = (
        inv_rms * (scaled - normed * jnp.mean(scaled * normed, axis=-1, keepdims=True))
    ).astype(jnp.bfloat16)
    near_dscores = jnp.where(
        near_mask, contract("cihd,cjhd->chij", out_grad, value_blocks), 0.0
    ).astype(jnp.bfloat16)
    far_dscores = jnp.where(
        far_mask, contract("cihd,cjhd->chij", out_grad, far_values), 0.0
    ).astype(jnp.bfloat16)
    state_grad = contract("cihk,cihd->chkd", query_blocks, out_grad)
    query_part = (
        contract("chij,cjhk->cihk", near_dscores, key_blocks)
        + contract("chij,cjhk->cihk", far_dscores, far_keys)
        + contract("cihd,chkd->cihk", out_grad, window_state)
    )
    key_near = contract("chij,cihk->cjhk", near_dscores, query_blocks)
    key_far = contract("chij,cihk->cjhk", far_dscores, query_blocks)
    value_near = contract("chij,cihd->cjhd", near_scores, out_grad)
    value_far = contract("chij,cihd->cjhd", far_scores, out_grad)
    return (query_part, key_near, key_far, value_near, value_far, state_grad, gain_part)


def finish(
    query_part,
    key_near,
    key_far_here,
    value_near,
    value_far_here,
    key_blocks,
    value_blocks,
    kv_grad,
):
    key_part = key_near + key_far_here + contract("cjhd,chkd->cjhk", value_blocks, kv_grad)
    value_part = value_near + value_far_here + contract("cjhk,chkd->cjhd", key_blocks, kv_grad)
    return (
        query_part.astype(jnp.bfloat16),
        key_part.astype(jnp.bfloat16),
        value_part.astype(jnp.bfloat16),
    )


def blocked(tensor, heads_count):
    return tensor[0, 0].reshape(-1, STRETCH, heads_count, HEAD_DIM)


GROUP = 2
MESH = pl.DeviceIdType.MESH
NN = (((1,), (0,)), ((), ()))
NT = (((1,), (1,)), ((), ()))
TN = (((0,), (0,)), ((), ()))


def dot(left, right, dims):
    return lax.dot_general(left, right, dims, preferred_element_type=jnp.float32)


def chain_kernel(
    n_ctx,
    n_dp,
    q_hbm,
    k_hbm,
    v_hbm,
    up_ref,
    gain_ref,
    qg_hbm,
    kg_hbm,
    vg_hbm,
    gg_ref,
    qg_ref,
    kg_ref,
    vg_ref,
    q_ref,
    k_ref,
    v_ref,
    g_buf,
    gain_all,
    gain_part,
    gain_stage,
    gain_mine,
    gain_final,
    kv_buf,
    near_buf,
    mix_buf,
    key_buf,
    val_buf,
    sg_buf,
    fwd_out,
    fwd_in,
    bwd_out,
    bwd_in,
    fwd_send,
    fwd_recv,
    bwd_send,
    bwd_recv,
    load_sem,
    store_sem,
    up_sem,
    gain_sem,
    stage_sem,
    final_sem,
):
    loads = [
        pltpu.make_async_copy(src, dst, load_sem.at[i])
        for i, (src, dst) in enumerate(((k_hbm, k_ref), (v_hbm, v_ref), (q_hbm, q_ref)))
    ]
    for load in loads:
        load.start()
    pipe = lax.axis_index("pipe")
    me = lax.axis_index("ctx")
    dp = lax.axis_index("dp")
    tokens, width = q_ref.shape
    heads = width // HEAD_DIM
    chunks = heads // GROUP
    per = width // n_ctx
    last = n_ctx - 1

    def at_ctx(c):
        return (pipe, c, dp)

    def at_dp(d):
        return (pipe, me, d)

    other = (1 - pipe, me, dp)
    ctx_peers = [lax.rem(me + o, n_ctx) for o in range(1, n_ctx)]
    dp_peers = [lax.rem(dp + o, n_dp) for o in range(1, n_dp)]

    barrier = pltpu.get_barrier_semaphore()
    pl.semaphore_signal(barrier, inc=1, device_id=other, device_id_type=MESH)
    for c in ctx_peers:
        pl.semaphore_signal(barrier, inc=1, device_id=at_ctx(c), device_id_type=MESH)
    for d in dp_peers:
        pl.semaphore_signal(barrier, inc=1, device_id=at_dp(d), device_id_type=MESH)

    def lanes(c, j):
        return pl.ds(pl.multiple_of((c * GROUP + j) * HEAD_DIM, HEAD_DIM), HEAD_DIM)

    def remote(src, dst, send, recv, target):
        return pltpu.make_async_remote_copy(
            src_ref=src,
            dst_ref=dst,
            send_sem=send,
            recv_sem=recv,
            device_id=target,
            device_id_type=MESH,
        )

    def fwd_copy(c, j):
        return remote(
            fwd_out.at[c, j],
            fwd_in.at[c, j],
            fwd_send.at[c, j],
            fwd_recv.at[c, j],
            at_ctx(jnp.minimum(me + 1, last)),
        )

    def bwd_copy(c, j):
        return remote(
            bwd_out.at[c, j],
            bwd_in.at[c, j],
            bwd_send.at[c, j],
            bwd_recv.at[c, j],
            at_ctx(jnp.maximum(me - 1, 0)),
        )

    @pl.when(me == 0)
    def _():
        fwd_in[...] = jnp.zeros_like(fwd_in)

    @pl.when(me == last)
    def _():
        bwd_in[...] = jnp.zeros_like(bwd_in)

    own_gain = pltpu.make_async_copy(gain_ref, gain_all.at[me], load_sem.at[3])
    own_gain.start()
    loads[0].wait()
    loads[1].wait()
    pl.semaphore_wait(barrier, 1 + len(ctx_peers) + len(dp_peers))

    def first(c, carry):
        for j in range(GROUP):
            at = lanes(c, j)
            kv = dot(k_ref[:, at], v_ref[:, at], TN)
            kv_buf[c, j] = kv
            fwd_out[c, j] = kv.astype(jnp.bfloat16)

        @pl.when(me == 0)
        def _():
            for j in range(GROUP):
                before = jnp.maximum(c * GROUP + j - DEPTH, 0)

                @pl.when(c * GROUP + j >= DEPTH)
                def _():
                    fwd_copy(before // GROUP, lax.rem(before, GROUP)).wait_send()

                fwd_copy(c, j).start()

        return carry

    up_copy = remote(up_ref, g_buf, up_sem.at[0], up_sem.at[1], other)
    up_copy.start()
    gain_copies = []
    for o, c in enumerate(ctx_peers):
        copy = remote(
            gain_ref, gain_all.at[me], gain_sem.at[0, o], gain_sem.at[1, o], at_ctx(c)
        )
        copy.start()
        gain_copies.append(copy)

    lax.fori_loop(0, chunks, first, 0)

    loads[2].wait()
    own_gain.wait()
    rows = lax.broadcasted_iota(jnp.int32, (tokens, tokens), 0)
    cols = lax.broadcasted_iota(jnp.int32, (tokens, tokens), 1)
    mask = rows >= cols

    def second(c, carry):
        for j in range(GROUP):
            at = lanes(c, j)
            near = jnp.where(mask, dot(q_ref[:, at], k_ref[:, at], NT), 0.0)
            near = near.astype(jnp.bfloat16)
            near_buf[c, j] = near
            mix_buf[c, j] = dot(near, v_ref[:, at], NN)
        return carry

    lax.fori_loop(0, chunks, second, 0)

    up_copy.wait()
    for copy in gain_copies:
        copy.wait()

    def store(which, c):
        source = (qg_ref, kg_ref, vg_ref)[which]
        target = (qg_hbm, kg_hbm, vg_hbm)[which]
        wide = GROUP * HEAD_DIM
        at = pl.ds(pl.multiple_of(c * wide, wide), wide)
        return pltpu.make_async_copy(source.at[:, at], target.at[:, at], store_sem.at[which, c])

    def forward(c):
        @pl.when(me == last)
        def _():
            for j in range(GROUP):
                fwd_copy(c, j).wait_recv()

        @pl.when(jnp.logical_and(me > 0, me < last))
        def _():
            for j in range(GROUP):
                fwd_copy(c, j).wait_recv()
                total = kv_buf[c, j] + fwd_in[c, j].astype(jnp.float32)
                fwd_out[c, j] = total.astype(jnp.bfloat16)
                fwd_copy(c, j).start()

        later = []
        for j in range(GROUP):
            at = lanes(c, j)
            query, state = q_ref[:, at], fwd_in[c, j]
            mixed = mix_buf[c, j] + dot(query, state, NN)
            inv_rms = lax.rsqrt(jnp.mean(mixed * mixed, axis=-1, keepdims=True) + 1e-06)
            normed = mixed * inv_rms
            grad = g_buf[:, at].astype(jnp.float32)
            place = (c * GROUP + j) * HEAD_DIM
            owner = place // per
            inside = pl.ds(pl.multiple_of(lax.rem(place, per), HEAD_DIM), HEAD_DIM)
            product = grad * normed
            gain_part[owner, :, inside] = jnp.sum(product, axis=0, keepdims=True)
            gain_row = gain_all[owner, :, inside]
            pull = jnp.mean(product * gain_row, axis=-1, keepdims=True)
            mixed_grad = (inv_rms * (grad * gain_row - normed * pull)).astype(jnp.bfloat16)
            state_grad = dot(query, mixed_grad, TN)
            sg_buf[c, j] = state_grad
            bwd_out[c, j] = state_grad.astype(jnp.bfloat16)
            later.append((at, query, state, mixed_grad))

        @pl.when(me == last)
        def _():
            for j in range(GROUP):
                bwd_copy(c, j).start()

        for j, (at, query, state, mixed_grad) in enumerate(later):
            near_grad = jnp.where(mask, dot(mixed_grad, v_ref[:, at], NT), 0.0)
            near_grad = near_grad.astype(jnp.bfloat16)
            query_grad = dot(near_grad, k_ref[:, at], NN) + dot(mixed_grad, state, NT)
            qg_ref[:, at] = query_grad.astype(jnp.bfloat16)
            key_buf[c, j] = dot(near_grad, query, TN)
            val_buf[c, j] = dot(near_buf[c, j], mixed_grad, TN)
        store(0, c).start()

    def backward(c):
        @pl.when(me == 0)
        def _():
            for j in range(GROUP):
                bwd_copy(c, j).wait_recv()

        @pl.when(jnp.logical_and(me > 0, me < last))
        def _():
            for j in range(GROUP):
                bwd_copy(c, j).wait_recv()
                total = sg_buf[c, j] + bwd_in[c, j].astype(jnp.float32)
                bwd_out[c, j] = total.astype(jnp.bfloat16)
                bwd_copy(c, j).start()

        for j in range(GROUP):
            at = lanes(c, j)
            kv_grad = bwd_in[c, j]
            key_grad = key_buf[c, j] + dot(v_ref[:, at], kv_grad, NT)
            kg_ref[:, at] = key_grad.astype(jnp.bfloat16)
            val_grad = val_buf[c, j] + dot(k_ref[:, at], kv_grad, NN)
            vg_ref[:, at] = val_grad.astype(jnp.bfloat16)
        store(1, c).start()
        store(2, c).start()

    def stage_copy(o):
        c = ctx_peers[o]
        return remote(
            gain_part.at[c], gain_stage.at[o], stage_sem.at[0, o], stage_sem.at[1, o], at_ctx(c)
        )

    def final_copy(o):
        return remote(
            gain_mine, gain_final.at[o], final_sem.at[0, o], final_sem.at[1, o], at_dp(dp_peers[o])
        )

    lag = jnp.minimum(chunks, (last - me) * LAG)
    steps = chunks + min(chunks, last * LAG)

    def step(i, carry):
        @pl.when(i < chunks)
        def _():
            forward(i)

        @pl.when(i == chunks - 1)
        def _():
            for o in range(n_ctx - 1):
                stage_copy(o).start()

        @pl.when(i == steps - 3)
        def _():
            total = gain_part[me]
            for o in range(n_ctx - 1):
                stage_copy(o).wait()
                total = total + gain_stage[o]
            gain_mine[...] = total
            for o in range(n_dp - 1):
                final_copy(o).start()

        @pl.when(jnp.logical_and(i >= lag, i - lag < chunks))
        def _():
            backward(i - lag)

        return carry

    lax.fori_loop(0, steps, step, 0)

    total = gain_mine[...]
    for o in range(n_dp - 1):
        final_copy(o).wait()
        total = total + gain_final[o]
    gain_mine[...] = total
    out_gain = pltpu.make_async_copy(gain_mine, gg_ref, load_sem.at[4])
    out_gain.start()
    for c in range(chunks):
        for which in range(3):
            store(which, c).wait()
    out_gain.wait()

    @pl.when(me < last)
    def _():
        for h in range(max(heads - DEPTH, 0), heads):
            fwd_copy(h // GROUP, h % GROUP).wait_send()

    @pl.when(jnp.logical_and(me > 0, me < last))
    def _():
        for h in range(heads - DEPTH):
            fwd_copy(h // GROUP, h % GROUP).wait_send()

    @pl.when(me > 0)
    def _():
        for c in range(chunks):
            for j in range(GROUP):
                bwd_copy(c, j).wait_send()


LAG = 4
DEPTH = 3
VMEM_BYTES = 63 * 1024 * 1024
PIECES = 4


def store_kernel(*refs):
    sources, targets, held, in_sems, out_sems = refs[:4], refs[4:8], refs[8:12], refs[12], refs[13]
    inward, outward = [], []
    for i in range(4):
        rows = sources[i].shape[0]
        pieces = PIECES if rows % (16 * PIECES) == 0 else 1
        for p in range(pieces):
            at = pl.ds(p * (rows // pieces), rows // pieces)
            here = held[i].at[at]
            inward.append(pltpu.make_async_copy(sources[i].at[at], here, in_sems.at[i, p]))
            outward.append(pltpu.make_async_copy(here, targets[i].at[at], out_sems.at[i, p]))
    for copy in inward:
        copy.start()
    for arrived, copy in zip(inward, outward):
        arrived.wait()
        copy.start()
    for copy in outward:
        copy.wait()


def chained(queries, keys, values, upstream, gain):
    n_ctx, n_dp = lax.axis_size("ctx"), lax.axis_size("dp")
    tokens, width = queries.shape[2:]
    heads = width // HEAD_DIM
    chunks = heads // GROUP
    per = gain.shape[1]
    wide = (chunks, GROUP, HEAD_DIM, HEAD_DIM)
    rows = (chunks, GROUP, tokens, HEAD_DIM)
    dma = pltpu.SemaphoreType.DMA
    token_out = jax.ShapeDtypeStruct((tokens, width), jnp.bfloat16)
    flat = [x.reshape(tokens, width) for x in (queries, keys, values, upstream)]
    hbm = pl.BlockSpec(memory_space=pltpu.HBM)
    shapes = (token_out, token_out, token_out, jax.ShapeDtypeStruct((1, per), jnp.float32))
    grads = pl.pallas_call(
        functools.partial(chain_kernel, n_ctx, n_dp),
        out_shape=shapes,
        in_specs=[hbm] * 5,
        out_specs=(hbm,) * 4,
        scratch_shapes=[
            pltpu.VMEM((tokens, width), jnp.bfloat16),
            pltpu.VMEM((tokens, width), jnp.bfloat16),
            pltpu.VMEM((tokens, width), jnp.bfloat16),
            pltpu.VMEM((tokens, width), jnp.bfloat16),
            pltpu.VMEM((tokens, width), jnp.bfloat16),
            pltpu.VMEM((tokens, width), jnp.bfloat16),
            pltpu.VMEM((tokens, width), jnp.bfloat16),
            pltpu.VMEM((n_ctx, 1, per), jnp.float32),
            pltpu.VMEM((n_ctx, 1, per), jnp.float32),
            pltpu.VMEM((n_ctx, 1, per), jnp.float32),
            pltpu.VMEM((1, per), jnp.float32),
            pltpu.VMEM((n_dp, 1, per), jnp.float32),
            pltpu.VMEM(wide, jnp.float32),
            pltpu.VMEM((chunks, GROUP, tokens, tokens), jnp.bfloat16),
            pltpu.VMEM(rows, jnp.float32),
            pltpu.VMEM(rows, jnp.float32),
            pltpu.VMEM(rows, jnp.float32),
            pltpu.VMEM(wide, jnp.float32),
            pltpu.VMEM(wide, jnp.bfloat16),
            pltpu.VMEM(wide, jnp.bfloat16),
            pltpu.VMEM(wide, jnp.bfloat16),
            pltpu.VMEM(wide, jnp.bfloat16),
            dma((chunks, GROUP)),
            dma((chunks, GROUP)),
            dma((chunks, GROUP)),
            dma((chunks, GROUP)),
            dma((5,)),
            dma((3, chunks)),
            dma((2,)),
            dma((2, n_ctx)),
            dma((2, n_ctx)),
            dma((2, n_dp)),
        ],
        compiler_params=pltpu.CompilerParams(
            collective_id=0, has_side_effects=True, vmem_limit_bytes=VMEM_BYTES
        ),
    )(*flat, gain)
    query_grad, key_grad, value_grad, gain_grad = pl.pallas_call(
        store_kernel,
        out_shape=shapes,
        in_specs=[hbm] * 4,
        out_specs=(hbm,) * 4,
        scratch_shapes=[pltpu.VMEM(x.shape, x.dtype) for x in shapes]
        + [dma((4, PIECES)), dma((4, PIECES))],
        compiler_params=pltpu.CompilerParams(vmem_limit_bytes=VMEM_BYTES),
    )(*grads)
    shape = queries.shape
    return (
        query_grad.reshape(shape),
        key_grad.reshape(shape),
        value_grad.reshape(shape),
        gain_grad,
    )


def shards(queries, keys, values, upstream, gain):
    reach_blocks = WINDOW // STRETCH
    if (
        queries.shape[2] == STRETCH
        and 1 < lax.axis_size("ctx") <= reach_blocks
        and lax.axis_size("pipe") == 2
    ):
        return chained(queries, keys, values, upstream, gain)
    incoming = shifted_2(upstream, "pipe", -1)
    heads_here = gain.shape[1] // HEAD_DIM
    query_heads, key_heads, value_heads, grad_heads = (
        lax.all_to_all(queries, "ctx", split_axis=3, concat_axis=2, tiled=True),
        lax.all_to_all(keys, "ctx", split_axis=3, concat_axis=2, tiled=True),
        lax.all_to_all(values, "ctx", split_axis=3, concat_axis=2, tiled=True),
        lax.all_to_all(incoming, "ctx", split_axis=3, concat_axis=2, tiled=True),
    )
    seq_len = query_heads.shape[2]
    gain_rows = gain[0].reshape(heads_here, HEAD_DIM)
    query_blocks = blocked(query_heads, heads_here)
    key_blocks = blocked(key_heads, heads_here)
    value_blocks = blocked(value_heads, heads_here)
    grad_blocks = blocked(grad_heads, heads_here)
    kv_stretches = contract("cshi,cshj->chij", key_blocks, value_blocks)
    prefix = shifted(jnp.cumsum(kv_stretches, axis=0), 1)
    window_state = (prefix - shifted(prefix, reach_blocks - 1)).astype(jnp.bfloat16)
    far_keys = shifted(key_blocks, reach_blocks)
    far_values = shifted(value_blocks, reach_blocks)
    query_part, key_near, key_far, value_near, value_far, state_grad, gain_part = local_grads(
        query_blocks,
        key_blocks,
        value_blocks,
        grad_blocks,
        far_keys,
        far_values,
        window_state,
        gain_rows,
    )
    later = lifted(jnp.flip(jnp.cumsum(jnp.flip(state_grad, 0), axis=0), 0), 1)
    kv_grad = (later - lifted(later, reach_blocks - 1)).astype(jnp.bfloat16)
    query_out, key_out, value_out = finish(
        query_part,
        key_near,
        lifted(key_far, reach_blocks),
        value_near,
        lifted(value_far, reach_blocks),
        key_blocks,
        value_blocks,
        kv_grad,
    )

    def head_rows(tensor):
        return tensor.reshape(1, 1, seq_len, heads_here * HEAD_DIM)

    query_grad, key_grad, value_grad = (
        lax.all_to_all(head_rows(query_out), "ctx", split_axis=2, concat_axis=3, tiled=True),
        lax.all_to_all(head_rows(key_out), "ctx", split_axis=2, concat_axis=3, tiled=True),
        lax.all_to_all(head_rows(value_out), "ctx", split_axis=2, concat_axis=3, tiled=True),
    )
    gain_share = gain_part.reshape(1, heads_here * HEAD_DIM)
    gain_total = lax.psum(gain_share, "dp")
    return (query_grad, key_grad, value_grad, gain_total)


def solution(mesh):
    in_specs = (
        P("pipe", "dp", "ctx", None),
        P("pipe", "dp", "ctx", None),
        P("pipe", "dp", "ctx", None),
        P("pipe", "dp", "ctx", None),
        P("pipe", "ctx"),
    )
    out_specs = (
        P("pipe", "dp", "ctx", None),
        P("pipe", "dp", "ctx", None),
        P("pipe", "dp", "ctx", None),
        P("pipe", "ctx"),
    )
    return jax.shard_map(shards, mesh=mesh, in_specs=in_specs, out_specs=out_specs, check_vma=False)
```

```python
import functools

import jax
import jax.numpy as jnp
from jax import lax
from jax.experimental import pallas as pl
from jax.experimental.pallas import tpu as pltpu
from jax.sharding import PartitionSpec as P

HEAD_DIM = 128
STRETCH = 128
WINDOW = 512


def shifted_2(array, axis, by):
    devices = lax.axis_size(axis)
    return lax.ppermute(array, axis, [(i, (i + by) % devices) for i in range(devices)])


def contract(form, left, right):
    return jnp.einsum(form, left, right, preferred_element_type=jnp.float32)


def shifted(tensor, amount):
    length = tensor.shape[0]
    amount = min(amount, length)
    filler = jnp.zeros((amount,) + tensor.shape[1:], tensor.dtype)
    return jnp.concatenate([filler, tensor[: length - amount]], axis=0)


def lifted(tensor, amount):
    length = tensor.shape[0]
    amount = min(amount, length)
    filler = jnp.zeros((amount,) + tensor.shape[1:], tensor.dtype)
    return jnp.concatenate([tensor[amount:], filler], axis=0)


def local_grads(
    query_blocks,
    key_blocks,
    value_blocks,
    grad_blocks,
    far_keys,
    far_values,
    window_state,
    gain_rows,
):
    rows_iota = lax.broadcasted_iota(jnp.int32, (STRETCH, STRETCH), 0)
    cols_iota = lax.broadcasted_iota(jnp.int32, (STRETCH, STRETCH), 1)
    near_mask = rows_iota >= cols_iota
    far_mask = rows_iota < cols_iota
    near_scores = jnp.where(
        near_mask, contract("cihk,cjhk->chij", query_blocks, key_blocks), 0.0
    ).astype(jnp.bfloat16)
    far_scores = jnp.where(
        far_mask, contract("cihk,cjhk->chij", query_blocks, far_keys), 0.0
    ).astype(jnp.bfloat16)
    mixed_out = (
        contract("chij,cjhd->cihd", near_scores, value_blocks)
        + contract("chij,cjhd->cihd", far_scores, far_values)
        + contract("cihk,chkd->cihd", query_blocks, window_state)
    )
    inv_rms = lax.rsqrt(jnp.mean(mixed_out * mixed_out, axis=-1, keepdims=True) + 1e-06)
    normed = mixed_out * inv_rms
    grad_float = grad_blocks.astype(jnp.float32)
    gain_part = jnp.sum(grad_float * normed, axis=(0, 1))
    scaled = grad_float * gain_rows
    out_grad = (
        inv_rms * (scaled - normed * jnp.mean(scaled * normed, axis=-1, keepdims=True))
    ).astype(jnp.bfloat16)
    near_dscores = jnp.where(
        near_mask, contract("cihd,cjhd->chij", out_grad, value_blocks), 0.0
    ).astype(jnp.bfloat16)
    far_dscores = jnp.where(
        far_mask, contract("cihd,cjhd->chij", out_grad, far_values), 0.0
    ).astype(jnp.bfloat16)
    state_grad = contract("cihk,cihd->chkd", query_blocks, out_grad)
    query_part = (
        contract("chij,cjhk->cihk", near_dscores, key_blocks)
        + contract("chij,cjhk->cihk", far_dscores, far_keys)
        + contract("cihd,chkd->cihk", out_grad, window_state)
    )
    key_near = contract("chij,cihk->cjhk", near_dscores, query_blocks)
    key_far = contract("chij,cihk->cjhk", far_dscores, query_blocks)
    value_near = contract("chij,cihd->cjhd", near_scores, out_grad)
    value_far = contract("chij,cihd->cjhd", far_scores, out_grad)
    return (query_part, key_near, key_far, value_near, value_far, state_grad, gain_part)


def finish(
    query_part,
    key_near,
    key_far_here,
    value_near,
    value_far_here,
    key_blocks,
    value_blocks,
    kv_grad,
):
    key_part = key_near + key_far_here + contract("cjhd,chkd->cjhk", value_blocks, kv_grad)
    value_part = value_near + value_far_here + contract("cjhk,chkd->cjhd", key_blocks, kv_grad)
    return (
        query_part.astype(jnp.bfloat16),
        key_part.astype(jnp.bfloat16),
        value_part.astype(jnp.bfloat16),
    )


def blocked(tensor, heads_count):
    return tensor[0, 0].reshape(-1, STRETCH, heads_count, HEAD_DIM)


GROUP = 2
MESH = pl.DeviceIdType.MESH
NN = (((1,), (0,)), ((), ()))
NT = (((1,), (1,)), ((), ()))
TN = (((0,), (0,)), ((), ()))


def dot(left, right, dims):
    return lax.dot_general(left, right, dims, preferred_element_type=jnp.float32)


def chain_kernel(
    n_ctx,
    n_dp,
    q_hbm,
    k_hbm,
    v_hbm,
    up_ref,
    gain_ref,
    qg_hbm,
    kg_hbm,
    vg_hbm,
    gg_ref,
    qg_ref,
    kg_ref,
    vg_ref,
    q_ref,
    k_ref,
    v_ref,
    g_buf,
    gain_all,
    gain_part,
    gain_stage,
    gain_mine,
    gain_final,
    kv_buf,
    near_buf,
    mix_buf,
    key_buf,
    val_buf,
    sg_buf,
    fwd_out,
    fwd_in,
    bwd_out,
    bwd_in,
    fwd_send,
    fwd_recv,
    bwd_send,
    bwd_recv,
    load_sem,
    store_sem,
    up_sem,
    gain_sem,
    stage_sem,
    final_sem,
):
    loads = [
        pltpu.make_async_copy(src, dst, load_sem.at[i])
        for i, (src, dst) in enumerate(((k_hbm, k_ref), (v_hbm, v_ref), (q_hbm, q_ref)))
    ]
    for load in loads:
        load.start()
    pipe = lax.axis_index("pipe")
    me = lax.axis_index("ctx")
    dp = lax.axis_index("dp")
    tokens, width = q_ref.shape
    heads = width // HEAD_DIM
    chunks = heads // GROUP
    per = width // n_ctx
    last = n_ctx - 1

    def at_ctx(c):
        return (pipe, c, dp)

    def at_dp(d):
        return (pipe, me, d)

    other = (1 - pipe, me, dp)
    ctx_peers = [lax.rem(me + o, n_ctx) for o in range(1, n_ctx)]
    dp_peers = [lax.rem(dp + o, n_dp) for o in range(1, n_dp)]

    barrier = pltpu.get_barrier_semaphore()
    pl.semaphore_signal(barrier, inc=1, device_id=other, device_id_type=MESH)
    for c in ctx_peers:
        pl.semaphore_signal(barrier, inc=1, device_id=at_ctx(c), device_id_type=MESH)
    for d in dp_peers:
        pl.semaphore_signal(barrier, inc=1, device_id=at_dp(d), device_id_type=MESH)

    def lanes(c, j):
        return pl.ds(pl.multiple_of((c * GROUP + j) * HEAD_DIM, HEAD_DIM), HEAD_DIM)

    def remote(src, dst, send, recv, target):
        return pltpu.make_async_remote_copy(
            src_ref=src,
            dst_ref=dst,
            send_sem=send,
            recv_sem=recv,
            device_id=target,
            device_id_type=MESH,
        )

    def fwd_copy(c, j):
        return remote(
            fwd_out.at[c, j],
            fwd_in.at[c, j],
            fwd_send.at[c, j],
            fwd_recv.at[c, j],
            at_ctx(jnp.minimum(me + 1, last)),
        )

    def bwd_copy(c, j):
        return remote(
            bwd_out.at[c, j],
            bwd_in.at[c, j],
            bwd_send.at[c, j],
            bwd_recv.at[c, j],
            at_ctx(jnp.maximum(me - 1, 0)),
        )

    @pl.when(me == 0)
    def _():
        fwd_in[...] = jnp.zeros_like(fwd_in)

    @pl.when(me == last)
    def _():
        bwd_in[...] = jnp.zeros_like(bwd_in)

    own_gain = pltpu.make_async_copy(gain_ref, gain_all.at[me], load_sem.at[3])
    own_gain.start()
    loads[0].wait()
    loads[1].wait()

    def first(c, carry):
        for j in range(GROUP):
            at = lanes(c, j)
            kv = dot(k_ref[:, at], v_ref[:, at], TN)
            kv_buf[c, j] = kv
            fwd_out[c, j] = kv.astype(jnp.bfloat16)
        return carry

    lax.fori_loop(0, chunks, first, 0)
    pl.semaphore_wait(barrier, 1 + len(ctx_peers) + len(dp_peers))

    def launch(c, carry):
        @pl.when(me == 0)
        def _():
            for j in range(GROUP):
                before = jnp.maximum(c * GROUP + j - DEPTH, 0)

                @pl.when(c * GROUP + j >= DEPTH)
                def _():
                    fwd_copy(before // GROUP, lax.rem(before, GROUP)).wait_send()

                fwd_copy(c, j).start()

        return carry

    up_copy = remote(up_ref, g_buf, up_sem.at[0], up_sem.at[1], other)
    up_copy.start()
    gain_copies = []
    for o, c in enumerate(ctx_peers):
        copy = remote(
            gain_ref, gain_all.at[me], gain_sem.at[0, o], gain_sem.at[1, o], at_ctx(c)
        )
        copy.start()
        gain_copies.append(copy)

    lax.fori_loop(0, chunks, launch, 0)

    loads[2].wait()
    own_gain.wait()
    rows = lax.broadcasted_iota(jnp.int32, (tokens, tokens), 0)
    cols = lax.broadcasted_iota(jnp.int32, (tokens, tokens), 1)
    mask = rows >= cols

    def second(c, carry):
        for j in range(GROUP):
            at = lanes(c, j)
            near = jnp.where(mask, dot(q_ref[:, at], k_ref[:, at], NT), 0.0)
            near = near.astype(jnp.bfloat16)
            near_buf[c, j] = near
            mix_buf[c, j] = dot(near, v_ref[:, at], NN)
        return carry

    lax.fori_loop(0, chunks, second, 0)

    up_copy.wait()
    for copy in gain_copies:
        copy.wait()

    def store(which, c):
        source = (qg_ref, kg_ref, vg_ref)[which]
        target = (qg_hbm, kg_hbm, vg_hbm)[which]
        wide = GROUP * HEAD_DIM
        at = pl.ds(pl.multiple_of(c * wide, wide), wide)
        return pltpu.make_async_copy(source.at[:, at], target.at[:, at], store_sem.at[which, c])

    def forward(c):
        @pl.when(me == last)
        def _():
            for j in range(GROUP):
                fwd_copy(c, j).wait_recv()

        @pl.when(jnp.logical_and(me > 0, me < last))
        def _():
            for j in range(GROUP):
                fwd_copy(c, j).wait_recv()
                total = kv_buf[c, j] + fwd_in[c, j].astype(jnp.float32)
                fwd_out[c, j] = total.astype(jnp.bfloat16)
                fwd_copy(c, j).start()

        later = []
        for j in range(GROUP):
            at = lanes(c, j)
            query, state = q_ref[:, at], fwd_in[c, j]
            mixed = mix_buf[c, j] + dot(query, state, NN)
            inv_rms = lax.rsqrt(jnp.mean(mixed * mixed, axis=-1, keepdims=True) + 1e-06)
            normed = mixed * inv_rms
            grad = g_buf[:, at].astype(jnp.float32)
            place = (c * GROUP + j) * HEAD_DIM
            owner = place // per
            inside = pl.ds(pl.multiple_of(lax.rem(place, per), HEAD_DIM), HEAD_DIM)
            product = grad * normed
            gain_part[owner, :, inside] = jnp.sum(product, axis=0, keepdims=True)
            gain_row = gain_all[owner, :, inside]
            pull = jnp.mean(product * gain_row, axis=-1, keepdims=True)
            mixed_grad = (inv_rms * (grad * gain_row - normed * pull)).astype(jnp.bfloat16)
            state_grad = dot(query, mixed_grad, TN)
            sg_buf[c, j] = state_grad
            bwd_out[c, j] = state_grad.astype(jnp.bfloat16)
            later.append((at, query, state, mixed_grad))

        @pl.when(me == last)
        def _():
            for j in range(GROUP):
                bwd_copy(c, j).start()

        for j, (at, query, state, mixed_grad) in enumerate(later):
            near_grad = jnp.where(mask, dot(mixed_grad, v_ref[:, at], NT), 0.0)
            near_grad = near_grad.astype(jnp.bfloat16)
            query_grad = dot(near_grad, k_ref[:, at], NN) + dot(mixed_grad, state, NT)
            qg_ref[:, at] = query_grad.astype(jnp.bfloat16)
            key_buf[c, j] = dot(near_grad, query, TN)
            val_buf[c, j] = dot(near_buf[c, j], mixed_grad, TN)
        store(0, c).start()

    def backward(c):
        @pl.when(me == 0)
        def _():
            for j in range(GROUP):
                bwd_copy(c, j).wait_recv()

        @pl.when(jnp.logical_and(me > 0, me < last))
        def _():
            for j in range(GROUP):
                bwd_copy(c, j).wait_recv()
                total = sg_buf[c, j] + bwd_in[c, j].astype(jnp.float32)
                bwd_out[c, j] = total.astype(jnp.bfloat16)
                bwd_copy(c, j).start()

        for j in range(GROUP):
            at = lanes(c, j)
            kv_grad = bwd_in[c, j]
            key_grad = key_buf[c, j] + dot(v_ref[:, at], kv_grad, NT)
            kg_ref[:, at] = key_grad.astype(jnp.bfloat16)
            val_grad = val_buf[c, j] + dot(k_ref[:, at], kv_grad, NN)
            vg_ref[:, at] = val_grad.astype(jnp.bfloat16)
        store(1, c).start()
        store(2, c).start()

    def stage_copy(o):
        c = ctx_peers[o]
        return remote(
            gain_part.at[c], gain_stage.at[o], stage_sem.at[0, o], stage_sem.at[1, o], at_ctx(c)
        )

    def final_copy(o):
        return remote(
            gain_mine, gain_final.at[o], final_sem.at[0, o], final_sem.at[1, o], at_dp(dp_peers[o])
        )

    lag = jnp.minimum(chunks, (last - me) * LAG)
    steps = chunks + min(chunks, last * LAG)

    def step(i, carry):
        @pl.when(i < chunks)
        def _():
            forward(i)

        @pl.when(i == chunks - 1)
        def _():
            for o in range(n_ctx - 1):
                stage_copy(o).start()

        @pl.when(i == steps - 3)
        def _():
            total = gain_part[me]
            for o in range(n_ctx - 1):
                stage_copy(o).wait()
                total = total + gain_stage[o]
            gain_mine[...] = total
            for o in range(n_dp - 1):
                final_copy(o).start()

        @pl.when(jnp.logical_and(i >= lag, i - lag < chunks))
        def _():
            backward(i - lag)

        return carry

    lax.fori_loop(0, steps, step, 0)

    total = gain_mine[...]
    for o in range(n_dp - 1):
        final_copy(o).wait()
        total = total + gain_final[o]
    gain_mine[...] = total
    out_gain = pltpu.make_async_copy(gain_mine, gg_ref, load_sem.at[4])
    out_gain.start()
    for c in range(chunks):
        for which in range(3):
            store(which, c).wait()
    out_gain.wait()

    @pl.when(me < last)
    def _():
        for h in range(max(heads - DEPTH, 0), heads):
            fwd_copy(h // GROUP, h % GROUP).wait_send()

    @pl.when(jnp.logical_and(me > 0, me < last))
    def _():
        for h in range(heads - DEPTH):
            fwd_copy(h // GROUP, h % GROUP).wait_send()

    @pl.when(me > 0)
    def _():
        for c in range(chunks):
            for j in range(GROUP):
                bwd_copy(c, j).wait_send()


LAG = 4
DEPTH = 3
VMEM_BYTES = 63 * 1024 * 1024
PIECES = 2


def store_kernel(*refs):
    sources, targets, held, in_sems, out_sems = refs[:4], refs[4:8], refs[8:12], refs[12], refs[13]
    inward, outward = [], []
    for i in range(4):
        rows = sources[i].shape[0]
        pieces = PIECES if rows % (16 * PIECES) == 0 else 1
        for p in range(pieces):
            at = pl.ds(p * (rows // pieces), rows // pieces)
            here = held[i].at[at]
            inward.append(pltpu.make_async_copy(sources[i].at[at], here, in_sems.at[i, p]))
            outward.append(pltpu.make_async_copy(here, targets[i].at[at], out_sems.at[i, p]))
    for copy in inward:
        copy.start()
    for arrived, copy in zip(inward, outward):
        arrived.wait()
        copy.start()
    for copy in outward:
        copy.wait()


def chained(queries, keys, values, upstream, gain):
    n_ctx, n_dp = lax.axis_size("ctx"), lax.axis_size("dp")
    tokens, width = queries.shape[2:]
    heads = width // HEAD_DIM
    chunks = heads // GROUP
    per = gain.shape[1]
    wide = (chunks, GROUP, HEAD_DIM, HEAD_DIM)
    rows = (chunks, GROUP, tokens, HEAD_DIM)
    dma = pltpu.SemaphoreType.DMA
    token_out = jax.ShapeDtypeStruct((tokens, width), jnp.bfloat16)
    flat = [x.reshape(tokens, width) for x in (queries, keys, values, upstream)]
    hbm = pl.BlockSpec(memory_space=pltpu.HBM)
    shapes = (token_out, token_out, token_out, jax.ShapeDtypeStruct((1, per), jnp.float32))
    grads = pl.pallas_call(
        functools.partial(chain_kernel, n_ctx, n_dp),
        out_shape=shapes,
        in_specs=[hbm] * 5,
        out_specs=(hbm,) * 4,
        scratch_shapes=[
            pltpu.VMEM((tokens, width), jnp.bfloat16),
            pltpu.VMEM((tokens, width), jnp.bfloat16),
            pltpu.VMEM((tokens, width), jnp.bfloat16),
            pltpu.VMEM((tokens, width), jnp.bfloat16),
            pltpu.VMEM((tokens, width), jnp.bfloat16),
            pltpu.VMEM((tokens, width), jnp.bfloat16),
            pltpu.VMEM((tokens, width), jnp.bfloat16),
            pltpu.VMEM((n_ctx, 1, per), jnp.float32),
            pltpu.VMEM((n_ctx, 1, per), jnp.float32),
            pltpu.VMEM((n_ctx, 1, per), jnp.float32),
            pltpu.VMEM((1, per), jnp.float32),
            pltpu.VMEM((n_dp, 1, per), jnp.float32),
            pltpu.VMEM(wide, jnp.float32),
            pltpu.VMEM((chunks, GROUP, tokens, tokens), jnp.bfloat16),
            pltpu.VMEM(rows, jnp.float32),
            pltpu.VMEM(rows, jnp.float32),
            pltpu.VMEM(rows, jnp.float32),
            pltpu.VMEM(wide, jnp.float32),
            pltpu.VMEM(wide, jnp.bfloat16),
            pltpu.VMEM(wide, jnp.bfloat16),
            pltpu.VMEM(wide, jnp.bfloat16),
            pltpu.VMEM(wide, jnp.bfloat16),
            dma((chunks, GROUP)),
            dma((chunks, GROUP)),
            dma((chunks, GROUP)),
            dma((chunks, GROUP)),
            dma((5,)),
            dma((3, chunks)),
            dma((2,)),
            dma((2, n_ctx)),
            dma((2, n_ctx)),
            dma((2, n_dp)),
        ],
        compiler_params=pltpu.CompilerParams(
            collective_id=0, has_side_effects=True, vmem_limit_bytes=VMEM_BYTES
        ),
    )(*flat, gain)
    query_grad, key_grad, value_grad, gain_grad = pl.pallas_call(
        store_kernel,
        out_shape=shapes,
        in_specs=[hbm] * 4,
        out_specs=(hbm,) * 4,
        scratch_shapes=[pltpu.VMEM(x.shape, x.dtype) for x in shapes]
        + [dma((4, PIECES)), dma((4, PIECES))],
        compiler_params=pltpu.CompilerParams(vmem_limit_bytes=VMEM_BYTES),
    )(*grads)
    shape = queries.shape
    return (
        query_grad.reshape(shape),
        key_grad.reshape(shape),
        value_grad.reshape(shape),
        gain_grad,
    )


def shards(queries, keys, values, upstream, gain):
    reach_blocks = WINDOW // STRETCH
    if (
        queries.shape[2] == STRETCH
        and 1 < lax.axis_size("ctx") <= reach_blocks
        and lax.axis_size("pipe") == 2
    ):
        return chained(queries, keys, values, upstream, gain)
    incoming = shifted_2(upstream, "pipe", -1)
    heads_here = gain.shape[1] // HEAD_DIM
    query_heads, key_heads, value_heads, grad_heads = (
        lax.all_to_all(queries, "ctx", split_axis=3, concat_axis=2, tiled=True),
        lax.all_to_all(keys, "ctx", split_axis=3, concat_axis=2, tiled=True),
        lax.all_to_all(values, "ctx", split_axis=3, concat_axis=2, tiled=True),
        lax.all_to_all(incoming, "ctx", split_axis=3, concat_axis=2, tiled=True),
    )
    seq_len = query_heads.shape[2]
    gain_rows = gain[0].reshape(heads_here, HEAD_DIM)
    query_blocks = blocked(query_heads, heads_here)
    key_blocks = blocked(key_heads, heads_here)
    value_blocks = blocked(value_heads, heads_here)
    grad_blocks = blocked(grad_heads, heads_here)
    kv_stretches = contract("cshi,cshj->chij", key_blocks, value_blocks)
    prefix = shifted(jnp.cumsum(kv_stretches, axis=0), 1)
    window_state = (prefix - shifted(prefix, reach_blocks - 1)).astype(jnp.bfloat16)
    far_keys = shifted(key_blocks, reach_blocks)
    far_values = shifted(value_blocks, reach_blocks)
    query_part, key_near, key_far, value_near, value_far, state_grad, gain_part = local_grads(
        query_blocks,
        key_blocks,
        value_blocks,
        grad_blocks,
        far_keys,
        far_values,
        window_state,
        gain_rows,
    )
    later = lifted(jnp.flip(jnp.cumsum(jnp.flip(state_grad, 0), axis=0), 0), 1)
    kv_grad = (later - lifted(later, reach_blocks - 1)).astype(jnp.bfloat16)
    query_out, key_out, value_out = finish(
        query_part,
        key_near,
        lifted(key_far, reach_blocks),
        value_near,
        lifted(value_far, reach_blocks),
        key_blocks,
        value_blocks,
        kv_grad,
    )

    def head_rows(tensor):
        return tensor.reshape(1, 1, seq_len, heads_here * HEAD_DIM)

    query_grad, key_grad, value_grad = (
        lax.all_to_all(head_rows(query_out), "ctx", split_axis=2, concat_axis=3, tiled=True),
        lax.all_to_all(head_rows(key_out), "ctx", split_axis=2, concat_axis=3, tiled=True),
        lax.all_to_all(head_rows(value_out), "ctx", split_axis=2, concat_axis=3, tiled=True),
    )
    gain_share = gain_part.reshape(1, heads_here * HEAD_DIM)
    gain_total = lax.psum(gain_share, "dp")
    return (query_grad, key_grad, value_grad, gain_total)


def solution(mesh):
    in_specs = (
        P("pipe", "dp", "ctx", None),
        P("pipe", "dp", "ctx", None),
        P("pipe", "dp", "ctx", None),
        P("pipe", "dp", "ctx", None),
        P("pipe", "ctx"),
    )
    out_specs = (
        P("pipe", "dp", "ctx", None),
        P("pipe", "dp", "ctx", None),
        P("pipe", "dp", "ctx", None),
        P("pipe", "ctx"),
    )
    return jax.shard_map(shards, mesh=mesh, in_specs=in_specs, out_specs=out_specs, check_vma=False)
```
